512 devices in a mesh: dp: 4 (over x), ctx: 128 (over y, z, core).
Axes of the slice: x: 4, y: 4, z: 16, core: 2. Of those that a mesh axis runs over, the one named last changes fastest.
Arguments:
- queries: bfloat16 [4, 16384, 8192], P('dp', 'ctx'), may hold values from -80 to 80
- grad_out: bfloat16 [4, 16384, 8192], P('dp', 'ctx'), may hold values from -6 to 6
- seq_lse: float32 [4, 16384, 64], P('dp', 'ctx'), may hold values from 4 to 10
- out_dot: float32 [4, 16384, 64], P('dp', 'ctx'), may hold values from -24 to 24
- prefix: bfloat16 [256, 2, 512], replicated, may hold values from -12 to 12
Outputs:
- updated: float32 [256, 2, 512], P('ctx')
The draws below stay inside these ranges and needn't reach their ends.
All inputs are finite; a program needn't handle non-finite values.
Results may differ from the reference program's by a relative error of at most 0.0013.
Values sent between devices are 32-bit elements; how exact they have to be, the bound alone decides.
No kernel may reach another device: no remote copies, remote signals or barrier semaphores. Data moves between devices by JAX's collectives and lax.ppermute only.
A program may use at most 64 MiB of HBM per device.

```python
import jax
import jax.numpy as jnp
from jax import lax

HEADS = 64
KV_HEADS = 4
HEAD = 128
PREFIX = 256
TOK_DEV = 128
GROUP = 16
TOKENS = 16384
DOCS = 4
N_CTX = 128


def prefix_rows(key):
    rows = jax.random.normal(jax.random.fold_in(key, 11), (PREFIX, KV_HEADS, HEAD), jnp.float32)
    return jnp.clip(rows, -4.0, 4.0)


def draw_prefix(key, part):
    keys = prefix_rows(key)
    key = jax.random.fold_in(key, 3)
    index = jnp.arange(PREFIX)
    rising = (1.0 + 2.0 * index / (PREFIX - 1.0))[:, None, None]
    values = jnp.clip(jax.random.normal(key, (PREFIX, KV_HEADS, HEAD), jnp.float32), -4.0, 4.0) * rising
    both = jnp.stack([keys.reshape(PREFIX, KV_HEADS * HEAD), values.reshape(PREFIX, KV_HEADS * HEAD)], 1)
    return both.astype(jnp.bfloat16)


def draw_queries(key, part):
    key = jax.random.fold_in(key, 7)
    shape = (DOCS, TOKENS, HEADS, HEAD)
    base = jnp.clip(jax.random.normal(key, shape, jnp.float32), -4.0, 4.0)
    return base.reshape(DOCS, TOKENS, HEADS * HEAD).astype(jnp.bfloat16)


def block_scale(own_key, extent, shards, smallest, high):
    loudness = 1.0
    for position, blocks in shards:
        heights = jax.random.uniform(jax.random.fold_in(jax.random.fold_in(own_key, 6), position), (blocks,), jnp.float32, smallest / len(shards), high / len(shards))
        loudness = loudness * jnp.repeat(jnp.exp(heights), extent[position] // blocks).reshape((-1,) + (1,) * (len(extent) - 1 - position))
    return loudness


def gaussian(rng, dims, width, most, split=(), held_as=jnp.bfloat16):
    result = width * jax.random.normal(rng, dims, jnp.float32)
    if split:
        result = result * block_scale(rng, dims, split, -0.22, 0.18)
    return jnp.clip(result, -most, most).astype(held_as)


def setup_inputs(seed: int = 0) -> dict:
    arg_keys = jax.random.split(jax.random.key(seed), 6)
    queries = draw_queries(jax.random.fold_in(arg_keys[5], 71), 0)
    grad_out = gaussian(arg_keys[1], (DOCS, TOKENS, HEADS * HEAD), 1.0, 6.0, ((0, 4), (1, 128)))
    seq_lse = jnp.clip(4.0 + 6.0 * jax.random.uniform(arg_keys[2], (DOCS, TOKENS, HEADS), jnp.float32) ** block_scale(arg_keys[2], (DOCS, TOKENS, HEADS), ((0, 4), (1, 128)), -0.2, 0.2), 4.0, 10.0)
    out_dot = gaussian(arg_keys[3], (DOCS, TOKENS, HEADS), 4.0, 24.0, ((0, 4), (1, 128)), jnp.float32)
    prefix = draw_prefix(jax.random.fold_in(arg_keys[5], 71), 0)
    return {"queries": queries, "grad_out": grad_out, "seq_lse": seq_lse, "out_dot": out_dot, "prefix": prefix}


def block_terms(q, dout, lse_seq, delta, keys, values):
    scale = HEAD ** (-0.5)
    scores = scale * jnp.einsum('rgjd,pgd->rgjp', q.astype(jnp.float32), keys.astype(jnp.float32))
    top = lax.optimization_barrier(jnp.max(scores, axis=-1))
    prefix_lse = top + jnp.log(lax.optimization_barrier(jnp.sum(jnp.exp(scores - top[..., None]), axis=-1)))
    total = jnp.logaddexp(lse_seq, prefix_lse)
    probs = jnp.exp(scores - total[..., None])
    probs_low = probs.astype(jnp.bfloat16)
    grad_v = jnp.einsum('rgjp,rgjd->pgd', probs_low.astype(jnp.float32), dout.astype(jnp.float32))
    dprobs = jnp.einsum('rgjd,pgd->rgjp', dout.astype(jnp.float32), values.astype(jnp.float32))
    dscores = (probs * (dprobs - delta[..., None])).astype(jnp.bfloat16)
    grad_k = scale * jnp.einsum('rgjp,rgjd->pgd', dscores.astype(jnp.float32), q.astype(jnp.float32))
    return (grad_k, grad_v)

def reference(queries, grad_out, seq_lse, out_dot, prefix):
    blocks = DOCS * N_CTX
    q_all = queries.reshape(blocks, TOK_DEV, KV_HEADS, GROUP, HEAD)
    d_all = grad_out.reshape(blocks, TOK_DEV, KV_HEADS, GROUP, HEAD)
    l_all = seq_lse.reshape(blocks, TOK_DEV, KV_HEADS, GROUP)
    o_all = out_dot.reshape(blocks, TOK_DEV, KV_HEADS, GROUP)
    keys = prefix[:, 0, :].reshape(PREFIX, KV_HEADS, HEAD)
    values = prefix[:, 1, :].reshape(PREFIX, KV_HEADS, HEAD)

    def step(carry, item):
        grad_k, grad_v = block_terms(item[0], item[1], item[2], item[3], keys, values)
        return ((carry[0] + grad_k, carry[1] + grad_v), None)
    start = jnp.zeros((PREFIX, KV_HEADS, HEAD), jnp.float32)
    (grad_k, grad_v), unused = lax.scan(step, (start, start), (q_all, d_all, l_all, o_all))
    grads = jnp.stack([grad_k.reshape(PREFIX, KV_HEADS * HEAD), grad_v.reshape(PREFIX, KV_HEADS * HEAD)], 1)
    weights = prefix.astype(jnp.float32)
    grad_ms = lax.optimization_barrier(jnp.mean(grads * grads, axis=(0, 2)))
    weight_ms = lax.optimization_barrier(jnp.mean(weights * weights, axis=(0, 2)))
    ratio = jnp.sqrt(weight_ms) / jnp.sqrt(grad_ms + 1e-06)
    return weights - 0.5 * ratio[None, :, None] * grads
```

```python
import jax
import jax.numpy as jnp
from jax import lax
from jax.sharding import Mesh, PartitionSpec as P

HEAD = 128


def local_grads(queries, grad_out, seq_lse, out_dot, prefix):
    kv_count = prefix.shape[2] // HEAD
    tok_rows = queries.shape[1]
    groups = queries.shape[2] // (kv_count * HEAD)
    rows_all = prefix.shape[0]
    scale = HEAD ** (-0.5)
    q_local = queries.reshape(tok_rows, kv_count, groups, HEAD)
    d_local = grad_out.reshape(tok_rows, kv_count, groups, HEAD)
    lse_local = seq_lse.reshape(tok_rows, kv_count, groups)
    delta = out_dot.reshape(tok_rows, kv_count, groups)
    keys = prefix[:, 0, :].reshape(rows_all, kv_count, HEAD)
    values = prefix[:, 1, :].reshape(rows_all, kv_count, HEAD)
    scores = scale * jnp.einsum("rgjd,pgd->rgjp", q_local, keys, preferred_element_type=jnp.float32)
    top = jnp.max(scores, axis=-1)
    prefix_lse = top + jnp.log(jnp.sum(jnp.exp(scores - top[..., None]), axis=-1))
    total = jnp.logaddexp(lse_local, prefix_lse)
    probs = jnp.exp(scores - total[..., None])
    probs_low = probs.astype(jnp.bfloat16)
    grad_v = jnp.einsum("rgjp,rgjd->pgd", probs_low, d_local, preferred_element_type=jnp.float32)
    dprobs = jnp.einsum("rgjd,pgd->rgjp", d_local, values, preferred_element_type=jnp.float32)
    dscores = (probs * (dprobs - delta[..., None])).astype(jnp.bfloat16)
    grad_k = scale * jnp.einsum(
        "rgjp,rgjd->pgd", dscores, q_local, preferred_element_type=jnp.float32
    )
    return grad_k, grad_v


def make_body(nx, ny, nz, nc):
    def body(queries, grad_out, seq_lse, out_dot, prefix):
        rows_all, width = prefix.shape[0], prefix.shape[2]
        own = rows_all // (ny * nz * nc)
        part = width // nx
        grad_k, grad_v = local_grads(queries, grad_out, seq_lse, out_dot, prefix)
        grads = jnp.stack([grad_k, grad_v], 0).reshape(2, ny, nz, nc, own, nx, part)
        grads = grads.transpose(3, 5, 1, 2, 0, 4, 6)
        core = lax.axis_index("c")
        mine = lax.dynamic_index_in_dim(grads, core, 0, keepdims=False)
        other = lax.dynamic_index_in_dim(grads, 1 - core, 0, keepdims=False)
        pairs = [(i, (i + 1) % nc) for i in range(nc)]
        half = mine + lax.ppermute(other, "c", pairs)
        rows = nz * 2 * own
        plane = lax.all_to_all(
            half.reshape(nx * ny, rows, part), ("x", "y"), 0, 0, tiled=True
        ).sum(0)
        piece = lax.all_to_all(
            plane.reshape(nz, 2 * own, part), "z", 0, 0, tiled=True
        ).sum(0)
        squares = (piece * piece).reshape(2, own, part).sum(1)
        squares = lax.all_to_all(
            jnp.broadcast_to(squares[None], (nz, 2, part)), "z", 0, 0, tiled=True
        ).sum(0)
        packed = jnp.concatenate([piece, squares], 0)
        count = nx * ny * nc
        packed = lax.all_to_all(
            jnp.broadcast_to(packed[None], (count,) + packed.shape),
            ("x", "y", "c"), 0, 0, tiled=True,
        )
        grad_ms = packed[:, 2 * own:].sum((0, 2)) / (rows_all * width)
        packed = packed.reshape(nx, ny * nc, 2 * own + 2, part)
        place = lax.axis_index("y") * nc + core
        mean = lax.dynamic_index_in_dim(packed, place, 1, keepdims=False)[:, : 2 * own]
        own_grads = mean.reshape(nx, 2, own, part).transpose(2, 1, 0, 3).reshape(own, 2, width)
        weights = prefix.astype(jnp.float32)
        weight_ms = jnp.mean(weights * weights, axis=(0, 2))
        ratio = jnp.sqrt(weight_ms) / jnp.sqrt(grad_ms + 1e-06)
        first = lax.axis_index(("y", "z", "c")) * own
        own_weights = lax.dynamic_slice_in_dim(weights, first, own, 0)
        return own_weights - 0.5 * ratio[None, :, None] * own_grads

    return body


def solution(mesh):
    nx, ny, nz, nc = mesh.shape["dp"], 4, 16, 2
    grid = Mesh(mesh.devices.reshape(nx, ny, nz, nc), ("x", "y", "z", "c"))
    tokens = P("x", ("y", "z", "c"), None)
    return jax.shard_map(
        make_body(nx, ny, nz, nc),
        mesh=grid,
        in_specs=(tokens, tokens, tokens, tokens, P()),
        out_specs=P(("y", "z", "c"), None, None),
        check_vma=False,
    )
```

```python
import functools

import jax
import jax.numpy as jnp
from jax import lax
from jax.experimental import pallas as pl
from jax.experimental.pallas import tpu as pltpu
from jax.sharding import Mesh, PartitionSpec as P

HEAD = 128
SCALE = HEAD ** (-0.5)
LOG2E = 1.4426950408889634
NT = (((1,), (1,)), ((), ()))
NN = (((1,), (0,)), ((), ()))
F32 = jnp.float32


def grads_kernel(
    ny, nz, core_ref, low_ref, q_ref, d_ref, lse_ref, dot_ref, send_ref, own_ref, sq_ref, w_ref
):
    group = pl.program_id(0)
    core = core_ref[0]
    heads = lse_ref.shape[0]

    @pl.when(group == 0)
    def _():
        w_ref[...] = low_ref[...].astype(F32)
        sq_ref[...] = jnp.zeros_like(sq_ref)

    sides = []
    for kv in range(2):
        rows = []
        total = jnp.zeros((8, HEAD), F32)
        for half in (1 - core, core):
            for y in range(ny):
                for r in range(2):
                    first = y * nz * 32 + half * 16 + r * 8 + group * 2 + kv
                    block = w_ref[pl.ds(first, nz, stride=32), :]
                    total += (block * block).reshape(nz // 8, 8, HEAD).sum(0)
                    rows.append(block)
        sides.append(jnp.concatenate(rows, 0).astype(jnp.bfloat16))
        sq_ref[kv] += total
    keys, values = sides

    q = jnp.concatenate([q_ref[:, h * HEAD : (h + 1) * HEAD] for h in range(heads)], 0)
    d = jnp.concatenate([d_ref[:, h * HEAD : (h + 1) * HEAD] for h in range(heads)], 0)
    lse = jnp.concatenate([lse_ref[h : h + 1, :] for h in range(heads)], 1) * LOG2E
    dot = jnp.concatenate([dot_ref[h : h + 1, :] for h in range(heads)], 1)
    scores = lax.dot_general(keys, q, NT, preferred_element_type=F32)
    top = jnp.maximum(jnp.max(scores, axis=0, keepdims=True) * (SCALE * LOG2E), lse)
    probs = jnp.exp2(scores * (SCALE * LOG2E) - top)
    probs = probs * (1.0 / (jnp.sum(probs, axis=0, keepdims=True) + jnp.exp2(lse - top)))
    dprobs = lax.dot_general(values, d, NT, preferred_element_type=F32)
    dscores = (probs * (dprobs - dot)).astype(jnp.bfloat16)
    grad_v = lax.dot_general(probs.astype(jnp.bfloat16), d, NN, preferred_element_type=F32)
    grad_k = lax.dot_general(dscores, q, NN, preferred_element_type=F32) * SCALE
    at = 0
    for ref in (send_ref, own_ref):
        for y in range(ny):
            for r in range(2):
                ref[0, y, pl.ds(r, nz, stride=4), :] = grad_k[at : at + nz]
                ref[0, y, pl.ds(2 + r, nz, stride=4), :] = grad_v[at : at + nz]
                at += nz


def local_grads(nx, ny, nz, core, weights, queries, grad_out, seq_lse, out_dot):
    tok, cols = queries.shape
    heads = seq_lse.shape[0] // nx
    half = jax.ShapeDtypeStruct((nx, ny, nz * 4, HEAD), F32)
    spec = pl.BlockSpec((1, ny, nz * 4, HEAD), lambda g: (g, 0, 0, 0))
    return pl.pallas_call(
        functools.partial(grads_kernel, ny, nz),
        grid=(nx,),
        in_specs=[
            pl.BlockSpec(memory_space=pltpu.SMEM),
            pl.BlockSpec(weights.shape, lambda g: (0, 0)),
            pl.BlockSpec((tok, cols // nx), lambda g: (0, g)),
            pl.BlockSpec((tok, cols // nx), lambda g: (0, g)),
            pl.BlockSpec((heads, tok), lambda g: (g, 0)),
            pl.BlockSpec((heads, tok), lambda g: (g, 0)),
        ],
        out_specs=[spec, spec, pl.BlockSpec((2, 8, HEAD), lambda g: (0, 0, 0))],
        out_shape=[half, half, jax.ShapeDtypeStruct((2, 8, HEAD), F32)],
        scratch_shapes=[pltpu.VMEM(weights.shape, F32)],
        compiler_params=pltpu.CompilerParams(vmem_limit_bytes=60 * 2**20),
        name="prefix_grads",
    )(core, weights, queries, grad_out, seq_lse, out_dot)


def make_body(nx, ny, nz, nc):
    def body(queries, grad_out, seq_lse, out_dot, prefix):
        rows_all, width = prefix.shape[0], prefix.shape[2]
        own = rows_all // (ny * nz * nc)
        part = width // nx
        core = lax.axis_index("c")
        weights = prefix.reshape(rows_all, 2, nx, part).transpose(0, 2, 1, 3).reshape(-1, part)
        send, mine, w_squares = local_grads(
            nx, ny, nz, core.reshape(1), weights, queries[0], grad_out[0], seq_lse[0].T, out_dot[0].T
        )
        half = mine + lax.ppermute(send, "c", [(i, (i + 1) % nc) for i in range(nc)])
        rows = nz * 2 * own
        plane = lax.all_to_all(
            half.reshape(nx * ny, rows, part), ("x", "y"), 0, 0, tiled=True
        ).sum(0)
        piece = lax.all_to_all(
            plane.reshape(nz, 2 * own, part), "z", 0, 0, tiled=True
        ).sum(0)
        squares = (piece * piece).reshape(2, own, part).sum(1)
        squares = lax.all_to_all(
            jnp.broadcast_to(squares[None], (nz, 2, part)), "z", 0, 0, tiled=True
        ).sum(0)
        packed = jnp.concatenate([piece, squares], 0)
        count = nx * ny * nc
        packed = lax.all_to_all(
            jnp.broadcast_to(packed[None], (count,) + packed.shape),
            ("x", "y", "c"), 0, 0, tiled=True,
        )
        grad_ms = packed[:, 2 * own :].sum((0, 2)) / (rows_all * width)
        packed = packed.reshape(nx, ny * nc, 2 * own + 2, part)
        place = lax.axis_index("y") * nc + core
        mean = lax.dynamic_index_in_dim(packed, place, 1, keepdims=False)[:, : 2 * own]
        own_grads = mean.reshape(nx, 2, own, part).transpose(2, 1, 0, 3).reshape(own, 2, width)
        weight_ms = w_squares.sum((1, 2)) / (rows_all * width)
        ratio = jnp.sqrt(weight_ms) / jnp.sqrt(grad_ms + 1e-06)
        first = lax.axis_index(("y", "z", "c")) * own
        own_weights = lax.dynamic_slice_in_dim(prefix, first, own, 0).astype(F32)
        return own_weights - 0.5 * ratio[None, :, None] * own_grads

    return body


def solution(mesh):
    nx, ny, nz, nc = mesh.shape["dp"], 4, 16, 2
    grid = Mesh(mesh.devices.reshape(nx, ny, nz, nc), ("x", "y", "z", "c"))
    tokens = P("x", ("y", "z", "c"), None)
    return jax.shard_map(
        make_body(nx, ny, nz, nc),
        mesh=grid,
        in_specs=(tokens, tokens, tokens, tokens, P()),
        out_specs=P(("y", "z", "c"), None, None),
        check_vma=False,
    )
```

```python
import functools

import jax
import jax.numpy as jnp
from jax import lax
from jax.experimental import pallas as pl
from jax.experimental.pallas import tpu as pltpu
from jax.sharding import Mesh, PartitionSpec as P

HEAD = 128
SCALE = HEAD ** (-0.5)
LOG2E = 1.4426950408889634
NT = (((1,), (1,)), ((), ()))
NN = (((1,), (0,)), ((), ()))
F32 = jnp.float32


def grads_kernel(
    ny, nz, at_ref, low_ref, q_ref, d_ref, lse_ref, dot_ref,
    send_ref, own_ref, sq_ref, own_w_ref, w_ref,
):
    group = pl.program_id(0)
    core = at_ref[0]
    heads = lse_ref.shape[0]

    @pl.when(group == 0)
    def _():
        w_ref[...] = low_ref[...].astype(F32)
        sq_ref[...] = jnp.zeros_like(sq_ref)
        start = pl.multiple_of(at_ref[1] * 8, 8)
        own_w_ref[...] = w_ref[pl.ds(start, own_w_ref.shape[0]), :]

    sides = []
    for kv in range(2):
        rows = []
        total = jnp.zeros((8, HEAD), F32)
        for half in (1 - core, core):
            for y in range(ny):
                for r in range(2):
                    first = y * nz * 32 + half * 16 + r * 8 + group * 2 + kv
                    block = w_ref[pl.ds(first, nz, stride=32), :]
                    total += (block * block).reshape(nz // 8, 8, HEAD).sum(0)
                    rows.append(block)
        sides.append(jnp.concatenate(rows, 0).astype(jnp.bfloat16))
        sq_ref[kv] += total
    keys, values = sides

    q = jnp.concatenate([q_ref[:, h * HEAD : (h + 1) * HEAD] for h in range(heads)], 0)
    d = jnp.concatenate([d_ref[:, h * HEAD : (h + 1) * HEAD] for h in range(heads)], 0)
    lse = jnp.concatenate([lse_ref[h : h + 1, :] for h in range(heads)], 1) * LOG2E
    dot = jnp.concatenate([dot_ref[h : h + 1, :] for h in range(heads)], 1)
    scores = lax.dot_general(keys, q, NT, preferred_element_type=F32)
    top = jnp.maximum(jnp.max(scores, axis=0, keepdims=True) * (SCALE * LOG2E), lse)
    probs = jnp.exp2(scores * (SCALE * LOG2E) - top)
    probs = probs * (1.0 / (jnp.sum(probs, axis=0, keepdims=True) + jnp.exp2(lse - top)))
    dprobs = lax.dot_general(values, d, NT, preferred_element_type=F32)
    dscores = (probs * (dprobs - dot)).astype(jnp.bfloat16)
    grad_v = lax.dot_general(probs.astype(jnp.bfloat16), d, NN, preferred_element_type=F32)
    grad_k = lax.dot_general(dscores, q, NN, preferred_element_type=F32) * SCALE
    at = 0
    for ref in (send_ref, own_ref):
        for y in range(ny):
            for r in range(2):
                ref[0, y, pl.ds(r, nz, stride=4), :] = grad_k[at : at + nz]
                ref[0, y, pl.ds(2 + r, nz, stride=4), :] = grad_v[at : at + nz]
                at += nz


def local_grads(nx, ny, nz, own, place, weights, queries, grad_out, seq_lse, out_dot):
    tok, cols = queries.shape
    heads = seq_lse.shape[0] // nx
    half = jax.ShapeDtypeStruct((nx, ny, nz * 4, HEAD), F32)
    spec = pl.BlockSpec((1, ny, nz * 4, HEAD), lambda g: (g, 0, 0, 0))
    return pl.pallas_call(
        functools.partial(grads_kernel, ny, nz),
        grid=(nx,),
        in_specs=[
            pl.BlockSpec(memory_space=pltpu.SMEM),
            pl.BlockSpec(weights.shape, lambda g: (0, 0)),
            pl.BlockSpec((tok, cols // nx), lambda g: (0, g)),
            pl.BlockSpec((tok, cols // nx), lambda g: (0, g)),
            pl.BlockSpec((heads, tok), lambda g: (g, 0)),
            pl.BlockSpec((heads, tok), lambda g: (g, 0)),
        ],
        out_specs=[
            spec,
            spec,
            pl.BlockSpec((2, 8, HEAD), lambda g: (0, 0, 0)),
            pl.BlockSpec((own * 8, HEAD), lambda g: (0, 0)),
        ],
        out_shape=[
            half,
            half,
            jax.ShapeDtypeStruct((2, 8, HEAD), F32),
            jax.ShapeDtypeStruct((own * 8, HEAD), F32),
        ],
        scratch_shapes=[pltpu.VMEM(weights.shape, F32)],
        compiler_params=pltpu.CompilerParams(vmem_limit_bytes=60 * 2**20),
        name="prefix_grads",
    )(place, weights, queries, grad_out, seq_lse, out_dot)


def make_body(nx, ny, nh, nl, nc):
    nz = nh * nl

    def exchange(block, axes):
        return lax.all_to_all(block, axes, 0, 0, tiled=True)

    def to_all(block, axes, count):
        return exchange(jnp.broadcast_to(block[None], (count,) + block.shape), axes)

    def body(queries, grad_out, seq_lse, out_dot, prefix):
        rows_all, width = prefix.shape[0], prefix.shape[2]
        own = rows_all // (ny * nz * nc)
        part = width // nx
        core = lax.axis_index("c")
        first = lax.axis_index(("y", "h", "l", "c")) * own
        weights = prefix.reshape(rows_all, 2, nx, part).transpose(0, 2, 1, 3).reshape(-1, part)
        send, mine, w_squares, own_weights = local_grads(
            nx, ny, nz, own, jnp.stack([core, first]), weights,
            queries[0], grad_out[0], seq_lse[0].T, out_dot[0].T,
        )
        half = mine + lax.ppermute(send, "c", [(i, (i + 1) % nc) for i in range(nc)])
        rows = 2 * own
        plane = exchange(half.reshape(nx * ny, nz * rows, part), ("x", "y")).sum(0)
        plane = plane.reshape(nh, nl, rows, part).transpose(1, 0, 2, 3)
        plane = jnp.broadcast_to(plane[None], (nh,) + plane.shape).reshape(nz, nh * rows, part)
        piece = exchange(plane, ("h", "l")).sum(0).reshape(nh, 2, own, part)
        squares = (piece * piece).sum((0, 2))
        piece = lax.dynamic_index_in_dim(piece, lax.axis_index("h"), 0, keepdims=False)
        packed = jnp.concatenate(
            [piece.reshape(rows, part), squares, jnp.zeros((8 - rows - 2, part), F32)], 0
        )
        packed = to_all(packed, ("x", "c"), nx * nc)
        squares = packed[:, rows : rows + 2].sum(0)
        packed = packed[:, :rows].reshape(nx, nc, 2, own, part)
        own_grads = lax.dynamic_index_in_dim(packed, core, 1, keepdims=False)
        grad_ms = to_all(squares, ("y", "l"), ny * nl).sum((0, 2)) / (rows_all * width)
        weight_ms = w_squares.sum((1, 2)) / (rows_all * width)
        ratio = jnp.sqrt(weight_ms) / jnp.sqrt(grad_ms + 1e-06)
        own_grads = own_grads.transpose(2, 1, 0, 3).reshape(own, 2, width)
        own_weights = own_weights.reshape(own, nx, 2, part).transpose(0, 2, 1, 3).reshape(own, 2, width)
        return own_weights - 0.5 * ratio[None, :, None] * own_grads

    return body


def solution(mesh):
    nx, ny, nh, nl, nc = mesh.shape["dp"], 4, 4, 4, 2
    grid = Mesh(mesh.devices.reshape(nx, ny, nh, nl, nc), ("x", "y", "h", "l", "c"))
    tokens = P("x", ("y", "h", "l", "c"), None)
    return jax.shard_map(
        make_body(nx, ny, nh, nl, nc),
        mesh=grid,
        in_specs=(tokens, tokens, tokens, tokens, P()),
        out_specs=P(("y", "h", "l", "c"), None, None),
        check_vma=False,
    )
```

```python
import functools

import jax
import jax.numpy as jnp
from jax import lax
from jax.experimental import pallas as pl
from jax.experimental.pallas import tpu as pltpu
from jax.sharding import Mesh, PartitionSpec as P

HEAD = 128
SCALE = HEAD ** (-0.5)
LOG2E = 1.4426950408889634
NT = (((1,), (1,)), ((), ()))
NN = (((1,), (0,)), ((), ()))
F32 = jnp.float32


def grads_kernel(
    ny, nz, core_ref, first_ref, low_ref, q_ref, d_ref, lse_ref, dot_ref,
    send_ref, own_ref, sq_ref, own_w_ref, w_ref,
):
    group = pl.program_id(0)
    core = core_ref[0]
    heads = lse_ref.shape[0]

    @pl.when(group == 0)
    def _():
        w_ref[...] = low_ref[...].astype(F32)
        sq_ref[...] = jnp.zeros_like(sq_ref)
        start = pl.multiple_of(first_ref[0] * 8, 8)
        own_w_ref[...] = w_ref[pl.ds(start, own_w_ref.shape[0]), :]

    sides = []
    for kv in range(2):
        rows = []
        total = jnp.zeros((8, HEAD), F32)
        for half in (1 - core, core):
            for y in range(ny):
                for r in range(2):
                    first = y * nz * 32 + half * 16 + r * 8 + group * 2 + kv
                    block = w_ref[pl.ds(first, nz, stride=32), :]
                    total += (block * block).reshape(nz // 8, 8, HEAD).sum(0)
                    rows.append(block)
        sides.append(jnp.concatenate(rows, 0).astype(jnp.bfloat16))
        sq_ref[kv] += total
    keys, values = sides

    q = jnp.concatenate([q_ref[:, h * HEAD : (h + 1) * HEAD] for h in range(heads)], 0)
    d = jnp.concatenate([d_ref[:, h * HEAD : (h + 1) * HEAD] for h in range(heads)], 0)
    lse = jnp.concatenate([lse_ref[h : h + 1, :] for h in range(heads)], 1) * LOG2E
    dot = jnp.concatenate([dot_ref[h : h + 1, :] for h in range(heads)], 1)
    scores = lax.dot_general(keys, q, NT, preferred_element_type=F32)
    top = jnp.maximum(jnp.max(scores, axis=0, keepdims=True) * (SCALE * LOG2E), lse)
    probs = jnp.exp2(scores * (SCALE * LOG2E) - top)
    probs = probs * (1.0 / (jnp.sum(probs, axis=0, keepdims=True) + jnp.exp2(lse - top)))
    dprobs = lax.dot_general(values, d, NT, preferred_element_type=F32)
    dscores = (probs * (dprobs - dot)).astype(jnp.bfloat16)
    grad_v = lax.dot_general(probs.astype(jnp.bfloat16), d, NN, preferred_element_type=F32)
    grad_k = lax.dot_general(dscores, q, NN, preferred_element_type=F32) * SCALE
    at = 0
    for ref in (send_ref, own_ref):
        for y in range(ny):
            for r in range(2):
                ref[0, y, pl.ds(r, nz, stride=4), :] = grad_k[at : at + nz]
                ref[0, y, pl.ds(2 + r, nz, stride=4), :] = grad_v[at : at + nz]
                at += nz


def local_grads(nx, ny, nz, own, core, first, weights, queries, grad_out, seq_lse, out_dot):
    tok, cols = queries.shape
    heads = seq_lse.shape[0] // nx
    half = jax.ShapeDtypeStruct((nx, ny, nz * 4, HEAD), F32)
    spec = pl.BlockSpec((1, ny, nz * 4, HEAD), lambda g: (g, 0, 0, 0))
    return pl.pallas_call(
        functools.partial(grads_kernel, ny, nz),
        grid=(nx,),
        in_specs=[
            pl.BlockSpec(memory_space=pltpu.SMEM),
            pl.BlockSpec(memory_space=pltpu.SMEM),
            pl.BlockSpec(weights.shape, lambda g: (0, 0)),
            pl.BlockSpec((tok, cols // nx), lambda g: (0, g)),
            pl.BlockSpec((tok, cols // nx), lambda g: (0, g)),
            pl.BlockSpec((heads, tok), lambda g: (g, 0)),
            pl.BlockSpec((heads, tok), lambda g: (g, 0)),
        ],
        out_specs=[
            spec,
            spec,
            pl.BlockSpec((2, 8, HEAD), lambda g: (0, 0, 0)),
            pl.BlockSpec((own * 8, HEAD), lambda g: (0, 0)),
        ],
        out_shape=[
            half,
            half,
            jax.ShapeDtypeStruct((2, 8, HEAD), F32),
            jax.ShapeDtypeStruct((own * 8, HEAD), F32),
        ],
        scratch_shapes=[pltpu.VMEM(weights.shape, F32)],
        compiler_params=pltpu.CompilerParams(vmem_limit_bytes=60 * 2**20),
        name="prefix_grads",
    )(core.reshape(1), first.reshape(1), weights, queries, grad_out, seq_lse, out_dot)


def make_body(nx, ny, nh, nl, nc):
    nz = nh * nl

    def exchange(block, axes):
        return lax.all_to_all(block, axes, 0, 0, tiled=True)

    def to_all(block, axes, count):
        return exchange(jnp.broadcast_to(block[None], (count,) + block.shape), axes)

    def body(queries, grad_out, seq_lse, out_dot, prefix):
        rows_all, width = prefix.shape[0], prefix.shape[2]
        own = rows_all // (ny * nz * nc)
        part = width // nx
        core = lax.axis_index("c")
        first = lax.axis_index(("y", "h", "l", "c")) * own
        weights = prefix.reshape(rows_all, 2, nx, part).transpose(0, 2, 1, 3).reshape(-1, part)
        send, mine, w_squares, own_weights = local_grads(
            nx, ny, nz, own, core, first, weights,
            queries[0], grad_out[0], seq_lse[0].T, out_dot[0].T,
        )
        half = mine + lax.ppermute(send, "c", [(i, (i + 1) % nc) for i in range(nc)])
        weight_ms = w_squares.sum((1, 2)) / (rows_all * width)
        at_h = lax.axis_index("h").astype(jnp.uint32)
        at_yl = lax.axis_index(("y", "l")).astype(jnp.uint32)
        half, weight_ms, own_weights, at_h, at_yl = lax.optimization_barrier(
            (half, weight_ms, own_weights, at_h, at_yl)
        )
        rows = 2 * own
        plane = exchange(half.reshape(nx * ny, nz * rows, part), ("x", "y")).sum(0)
        plane = plane.reshape(nh, nl, rows, part).transpose(1, 0, 2, 3)
        plane = jnp.broadcast_to(plane[None], (nh,) + plane.shape).reshape(nz, nh * rows, part)
        piece = exchange(plane, ("h", "l")).sum(0).reshape(nh, 2, own, part)
        squares = lax.all_gather((piece * piece).sum((0, 2)), "c").sum(0)
        squares = squares.reshape(2, 2, part // 2).sum(1).reshape(1, part)
        piece = lax.dynamic_index_in_dim(piece, at_h, 0, keepdims=False)
        packed = jnp.concatenate([piece.reshape(rows, part), squares], 0).reshape(1, -1)
        packed = to_all(packed, ("x", "y", "l"), nx * ny * nl)
        grad_ms = packed[:, 0, rows * part :].reshape(-1, 2, part // 2).sum((0, 2)) / (rows_all * width)
        packed = packed.reshape(nx, ny * nl, -1)
        own_grads = lax.dynamic_index_in_dim(packed, at_yl, 1, keepdims=False)[:, : rows * part]
        own_grads = own_grads.reshape(nx, 2, own, part).transpose(2, 1, 0, 3).reshape(own, 2, width)
        ratio = jnp.sqrt(weight_ms) / jnp.sqrt(grad_ms + 1e-06)
        own_weights = own_weights.reshape(own, nx, 2, part).transpose(0, 2, 1, 3).reshape(own, 2, width)
        return own_weights - 0.5 * ratio[None, :, None] * own_grads

    return body


def solution(mesh):
    nx, ny, nh, nl, nc = mesh.shape["dp"], 4, 4, 4, 2
    grid = Mesh(mesh.devices.reshape(nx, ny, nh, nl, nc), ("x", "y", "h", "l", "c"))
    tokens = P("x", ("y", "h", "l", "c"), None)
    return jax.shard_map(
        make_body(nx, ny, nh, nl, nc),
        mesh=grid,
        in_specs=(tokens, tokens, tokens, tokens, P()),
        out_specs=P(("y", "h", "l", "c"), None, None),
        check_vma=False,
    )
```

```python
import functools

import jax
import jax.numpy as jnp
from jax import lax
from jax.experimental import pallas as pl
from jax.experimental.pallas import tpu as pltpu
from jax.sharding import Mesh, PartitionSpec as P

HEAD = 128
SCALE = HEAD ** (-0.5)
LOG2E = 1.4426950408889634
NT = (((1,), (1,)), ((), ()))
NN = (((1,), (0,)), ((), ()))
F32 = jnp.float32


def grads_kernel(
    ny, nz, core_ref, first_ref, low_hbm, q_hbm, d_hbm, lse_hbm, dot_hbm,
    send_ref, own_ref, sq_ref, own_w_ref,
    low_ref, q_ref, d_ref, lse_ref, dot_ref, w_ref, low_sem, row_sem, q_sem, d_sem,
):
    core = core_ref[0]
    groups, _, cols = q_ref.shape
    heads = cols // HEAD
    prefix_copy = pltpu.make_async_copy(low_hbm, low_ref, low_sem)
    row_copies = [
        pltpu.make_async_copy(lse_hbm, lse_ref, row_sem.at[0]),
        pltpu.make_async_copy(dot_hbm, dot_ref, row_sem.at[1]),
    ]

    def copies(g):
        span = pl.ds(g * cols, cols)
        return [
            pltpu.make_async_copy(q_hbm.at[:, span], q_ref.at[g], q_sem.at[g]),
            pltpu.make_async_copy(d_hbm.at[:, span], d_ref.at[g], d_sem.at[g]),
        ]

    prefix_copy.start()
    for copy in copies(0) + row_copies:
        copy.start()
    prefix_copy.wait()
    w_ref[...] = low_ref[...].astype(F32)
    start = pl.multiple_of(first_ref[0] * 8, 8)
    own_w_ref[...] = w_ref[pl.ds(start, own_w_ref.shape[0]), :]

    sides = []
    total = [jnp.zeros((8, HEAD), F32)] * 2
    for g in range(groups):
        for kv in range(2):
            rows = []
            for half in (1 - core, core):
                for y in range(ny):
                    for r in range(2):
                        first = y * nz * 32 + half * 16 + r * 8 + g * 2 + kv
                        block = w_ref[pl.ds(first, nz, stride=32), :]
                        total[kv] += (block * block).reshape(nz // 8, 8, HEAD).sum(0)
                        rows.append(block)
            sides.append(jnp.concatenate(rows, 0).astype(jnp.bfloat16))
    for kv in range(2):
        sq_ref[kv] = total[kv]
    for copy in row_copies:
        copy.wait()

    def rows_of(ref, g):
        return jnp.concatenate([ref[g, :, h * HEAD : (h + 1) * HEAD] for h in range(heads)], 0)

    def line_of(ref, g):
        return jnp.concatenate([ref[g * heads + h : g * heads + h + 1, :] for h in range(heads)], 1)

    def products(g):
        for copy in copies(g):
            copy.wait()
        if g + 1 < groups:
            for copy in copies(g + 1):
                copy.start()
        scores = lax.dot_general(sides[2 * g], rows_of(q_ref, g), NT, preferred_element_type=F32)
        dprobs = lax.dot_general(sides[2 * g + 1], rows_of(d_ref, g), NT, preferred_element_type=F32)
        return scores, dprobs

    def weights_of(g, scores, dprobs):
        lse = line_of(lse_ref, g) * LOG2E
        top = jnp.maximum(jnp.max(scores, axis=0, keepdims=True) * (SCALE * LOG2E), lse)
        probs = jnp.exp2(scores * (SCALE * LOG2E) - top)
        probs = probs * (1.0 / (jnp.sum(probs, axis=0, keepdims=True) + jnp.exp2(lse - top)))
        dscores = probs * (dprobs - line_of(dot_ref, g))
        return probs.astype(jnp.bfloat16), dscores.astype(jnp.bfloat16)

    def finish(g, probs, dscores):
        grad_v = lax.dot_general(probs, rows_of(d_ref, g), NN, preferred_element_type=F32)
        grad_k = lax.dot_general(dscores, rows_of(q_ref, g), NN, preferred_element_type=F32) * SCALE
        at = 0
        for ref in (send_ref, own_ref):
            for y in range(ny):
                for r in range(2):
                    ref[g, y, pl.ds(r, nz, stride=4), :] = grad_k[at : at + nz]
                    ref[g, y, pl.ds(2 + r, nz, stride=4), :] = grad_v[at : at + nz]
                    at += nz

    for g in range(groups - 1):
        finish(g, *weights_of(g, *products(g)))
    held = weights_of(groups - 1, *products(groups - 1))
    finish(groups - 1, *held)


def local_grads(nx, ny, nz, own, core, first, weights, queries, grad_out, seq_lse, out_dot):
    tok, cols = queries.shape
    half = jax.ShapeDtypeStruct((nx, ny, nz * 4, HEAD), F32)
    vmem = pl.BlockSpec(memory_space=pltpu.VMEM)
    smem = pl.BlockSpec(memory_space=pltpu.SMEM)
    hbm = pl.BlockSpec(memory_space=pltpu.HBM)
    operands = [weights, queries, grad_out, seq_lse, out_dot]
    operands = [pltpu.with_memory_space_constraint(x, pltpu.HBM) for x in operands]
    return pl.pallas_call(
        functools.partial(grads_kernel, ny, nz),
        in_specs=[smem, smem] + [hbm] * 5,
        out_specs=[vmem] * 4,
        out_shape=[half, half, jax.ShapeDtypeStruct((2, 8, HEAD), F32), jax.ShapeDtypeStruct((own * 8, HEAD), F32)],
        scratch_shapes=[
            pltpu.VMEM(weights.shape, weights.dtype),
            pltpu.VMEM((nx, tok, cols // nx), queries.dtype),
            pltpu.VMEM((nx, tok, cols // nx), grad_out.dtype),
            pltpu.VMEM(seq_lse.shape, F32),
            pltpu.VMEM(out_dot.shape, F32),
            pltpu.VMEM(weights.shape, F32),
            pltpu.SemaphoreType.DMA,
            pltpu.SemaphoreType.DMA((2,)),
            pltpu.SemaphoreType.DMA((nx,)),
            pltpu.SemaphoreType.DMA((nx,)),
        ],
        compiler_params=pltpu.CompilerParams(vmem_limit_bytes=40 * 2**20),
        name="prefix_grads",
    )(core.reshape(1), first.reshape(1), *operands)


def make_body(nx, ny, nh, nl, nc):
    nz = nh * nl

    def exchange(block, axes):
        return lax.all_to_all(block, axes, 0, 0, tiled=True)

    def to_all(block, axes, count):
        return exchange(jnp.broadcast_to(block[None], (count,) + block.shape), axes)

    def body(queries, grad_out, seq_lse, out_dot, prefix):
        rows_all, width = prefix.shape[0], prefix.shape[2]
        own = rows_all // (ny * nz * nc)
        part = width // nx
        core = lax.axis_index("c")
        first = lax.axis_index(("y", "h", "l", "c")) * own
        weights = prefix.reshape(rows_all, 2, nx, part).transpose(0, 2, 1, 3).reshape(-1, part)
        send, mine, w_squares, own_weights = local_grads(
            nx, ny, nz, own, core, first, weights,
            queries[0], grad_out[0], seq_lse[0].T, out_dot[0].T,
        )
        half = mine + lax.ppermute(send, "c", [(i, (i + 1) % nc) for i in range(nc)])
        weight_ms = w_squares.sum((1, 2)) / (rows_all * width)
        at_h = lax.axis_index("h").astype(jnp.uint32)
        at_yl = lax.axis_index(("y", "l")).astype(jnp.uint32)
        half, weight_ms, own_weights, at_h, at_yl = lax.optimization_barrier(
            (half, weight_ms, own_weights, at_h, at_yl)
        )
        rows = 2 * own
        plane = exchange(half.reshape(nx * ny, nz * rows, part), ("x", "y")).sum(0)
        plane = plane.reshape(nh, nl, rows, part).transpose(1, 0, 2, 3)
        plane = jnp.broadcast_to(plane[None], (nh,) + plane.shape).reshape(nz, nh * rows, part)
        piece = exchange(plane, ("h", "l")).sum(0).reshape(nh, 2, own, part)
        squares = lax.all_gather((piece * piece).sum((0, 2)), "c").sum(0)
        squares = squares.reshape(2, 2, part // 2).sum(1).reshape(1, part)
        piece = lax.dynamic_index_in_dim(piece, at_h, 0, keepdims=False)
        packed = jnp.concatenate([piece.reshape(rows, part), squares], 0).reshape(1, -1)
        packed = to_all(packed, ("x", "y", "l"), nx * ny * nl)
        grad_ms = packed[:, 0, rows * part :].reshape(-1, 2, part // 2).sum((0, 2)) / (rows_all * width)
        packed = packed.reshape(nx, ny * nl, -1)
        own_grads = lax.dynamic_index_in_dim(packed, at_yl, 1, keepdims=False)[:, : rows * part]
        own_grads = own_grads.reshape(nx, 2, own, part).transpose(2, 1, 0, 3).reshape(own, 2, width)
        ratio = jnp.sqrt(weight_ms) / jnp.sqrt(grad_ms + 1e-06)
        own_weights = own_weights.reshape(own, nx, 2, part).transpose(0, 2, 1, 3).reshape(own, 2, width)
        return own_weights - 0.5 * ratio[None, :, None] * own_grads

    return body


def solution(mesh):
    nx, ny, nh, nl, nc = mesh.shape["dp"], 4, 4, 4, 2
    grid = Mesh(mesh.devices.reshape(nx, ny, nh, nl, nc), ("x", "y", "h", "l", "c"))
    tokens = P("x", ("y", "h", "l", "c"), None)
    return jax.shard_map(
        make_body(nx, ny, nh, nl, nc),
        mesh=grid,
        in_specs=(tokens, tokens, tokens, tokens, P()),
        out_specs=P(("y", "h", "l", "c"), None, None),
        check_vma=False,
    )
```

```python
import functools

import jax
import jax.numpy as jnp
from jax import lax
from jax.experimental import pallas as pl
from jax.experimental.pallas import tpu as pltpu
from jax.sharding import Mesh, PartitionSpec as P

HEAD = 128
SCALE = HEAD ** (-0.5)
LOG2E = 1.4426950408889634
NT = (((1,), (1,)), ((), ()))
NN = (((1,), (0,)), ((), ()))
F32 = jnp.float32


def grads_kernel(
    ny, nz, core_ref, first_ref, low_hbm, q_hbm, d_hbm, lse_hbm, dot_hbm,
    send_ref, own_ref, sq_ref, own_w_ref,
    low_ref, q_ref, d_ref, lse_ref, dot_ref, w_ref, low_sem, row_sem, q_sem, d_sem,
):
    core = core_ref[0]
    groups, _, cols = q_ref.shape
    heads = cols // HEAD
    prefix_copy = pltpu.make_async_copy(low_hbm, low_ref, low_sem)
    row_copies = [
        pltpu.make_async_copy(lse_hbm, lse_ref, row_sem.at[0]),
        pltpu.make_async_copy(dot_hbm, dot_ref, row_sem.at[1]),
    ]

    def copies(g):
        span = pl.ds(g * cols, cols)
        return [
            pltpu.make_async_copy(q_hbm.at[:, span], q_ref.at[g], q_sem.at[g]),
            pltpu.make_async_copy(d_hbm.at[:, span], d_ref.at[g], d_sem.at[g]),
        ]

    prefix_copy.start()
    for copy in copies(0) + row_copies:
        copy.start()
    prefix_copy.wait()
    w_ref[...] = low_ref[...].astype(F32)
    start = pl.multiple_of(first_ref[0] * 8, 8)
    own_w_ref[...] = w_ref[pl.ds(start, own_w_ref.shape[0]), :]

    def gather(g, kv):
        rows = []
        for half in (1 - core, core):
            for y in range(ny):
                for r in range(2):
                    first = y * nz * 32 + half * 16 + r * 8 + g * 2 + kv
                    rows.append(w_ref[pl.ds(first, nz, stride=32), :])
        return jnp.concatenate(rows, 0)

    def rows_of(ref, g):
        return jnp.concatenate([ref[g, :, h * HEAD : (h + 1) * HEAD] for h in range(heads)], 0)

    def line_of(ref, g):
        lines = ref[pl.ds(g * heads, heads), :]
        return jnp.concatenate([lines[h : h + 1, :] for h in range(heads)], 1)

    def group(g, keys, values, stable):
        scores = lax.dot_general(keys, rows_of(q_ref, g), NT, preferred_element_type=F32)
        dprobs = lax.dot_general(values, rows_of(d_ref, g), NT, preferred_element_type=F32)
        lse = line_of(lse_ref, g) * LOG2E
        top = lse
        if stable:
            top = jnp.maximum(jnp.max(scores, axis=0, keepdims=True) * (SCALE * LOG2E), lse)
        probs = jnp.exp2(scores * (SCALE * LOG2E) - top)
        total = jnp.sum(probs, axis=0, keepdims=True)
        probs = probs * (1.0 / (total + (jnp.exp2(lse - top) if stable else 1.0)))
        dscores = (probs * (dprobs - line_of(dot_ref, g))).astype(jnp.bfloat16)
        probs = probs.astype(jnp.bfloat16)
        grad_v = lax.dot_general(probs, rows_of(d_ref, g), NN, preferred_element_type=F32)
        grad_k = lax.dot_general(dscores, rows_of(q_ref, g), NN, preferred_element_type=F32) * SCALE
        at = 0
        for ref in (send_ref, own_ref):
            for y in range(ny):
                for r in range(2):
                    ref[g, y, pl.ds(r, nz, stride=4), :] = grad_k[at : at + nz]
                    ref[g, y, pl.ds(2 + r, nz, stride=4), :] = grad_v[at : at + nz]
                    at += nz
        return total

    sides = []
    for kv in range(2):
        sides.append([gather(g, kv) for g in range(groups)])
        sq_ref[kv] = sum((x * x).reshape(-1, 8, HEAD).sum(0) for x in sides[kv])
    for copy in row_copies:
        copy.wait()
    peak = None
    for g in range(groups):
        for copy in copies(g):
            copy.wait()
        if g + 1 < groups:
            for copy in copies(g + 1):
                copy.start()
        keys, values = (sides[kv][g].astype(jnp.bfloat16) for kv in range(2))
        total = group(g, keys, values, False)
        peak = total if peak is None else jnp.maximum(peak, total)

    @pl.when(jnp.max(peak) > 2.0**100)
    def _():
        def again(g, carry):
            group(g, gather(g, 0).astype(jnp.bfloat16), gather(g, 1).astype(jnp.bfloat16), True)
            return carry

        lax.fori_loop(0, groups, again, 0)


def local_grads(nx, ny, nz, own, core, first, weights, queries, grad_out, seq_lse, out_dot):
    tok, cols = queries.shape
    half = jax.ShapeDtypeStruct((nx, ny, nz * 4, HEAD), F32)
    vmem = pl.BlockSpec(memory_space=pltpu.VMEM)
    smem = pl.BlockSpec(memory_space=pltpu.SMEM)
    hbm = pl.BlockSpec(memory_space=pltpu.HBM)
    operands = [weights, queries, grad_out, seq_lse, out_dot]
    operands = [pltpu.with_memory_space_constraint(x, pltpu.HBM) for x in operands]
    return pl.pallas_call(
        functools.partial(grads_kernel, ny, nz),
        in_specs=[smem, smem] + [hbm] * 5,
        out_specs=[vmem] * 4,
        out_shape=[half, half, jax.ShapeDtypeStruct((2, 8, HEAD), F32), jax.ShapeDtypeStruct((own * 8, HEAD), F32)],
        scratch_shapes=[
            pltpu.VMEM(weights.shape, weights.dtype),
            pltpu.VMEM((nx, tok, cols // nx), queries.dtype),
            pltpu.VMEM((nx, tok, cols // nx), grad_out.dtype),
            pltpu.VMEM(seq_lse.shape, F32),
            pltpu.VMEM(out_dot.shape, F32),
            pltpu.VMEM(weights.shape, F32),
            pltpu.SemaphoreType.DMA,
            pltpu.SemaphoreType.DMA((2,)),
            pltpu.SemaphoreType.DMA((nx,)),
            pltpu.SemaphoreType.DMA((nx,)),
        ],
        compiler_params=pltpu.CompilerParams(vmem_limit_bytes=40 * 2**20),
        name="prefix_grads",
    )(core.reshape(1), first.reshape(1), *operands)


def make_body(nx, ny, nh, nl, nc):
    nz = nh * nl

    def exchange(block, axes):
        return lax.all_to_all(block, axes, 0, 0, tiled=True)

    def to_all(block, axes, count):
        return exchange(jnp.broadcast_to(block[None], (count,) + block.shape), axes)

    def body(queries, grad_out, seq_lse, out_dot, prefix):
        rows_all, width = prefix.shape[0], prefix.shape[2]
        own = rows_all // (ny * nz * nc)
        part = width // nx
        core = lax.axis_index("c")
        first = lax.axis_index(("y", "h", "l", "c")) * own
        weights = prefix.reshape(rows_all, 2, nx, part).transpose(0, 2, 1, 3).reshape(-1, part)
        send, mine, w_squares, own_weights = local_grads(
            nx, ny, nz, own, core, first, weights,
            queries[0], grad_out[0], seq_lse[0].T, out_dot[0].T,
        )
        half = mine + lax.ppermute(send, "c", [(i, (i + 1) % nc) for i in range(nc)])
        weight_ms = w_squares.sum((1, 2)) / (rows_all * width)
        at_h = lax.axis_index("h").astype(jnp.uint32)
        at_yl = lax.axis_index(("y", "l")).astype(jnp.uint32)
        half, weight_ms, own_weights, at_h, at_yl = lax.optimization_barrier(
            (half, weight_ms, own_weights, at_h, at_yl)
        )
        rows = 2 * own
        plane = exchange(half.reshape(nx * ny, nz * rows, part), ("x", "y")).sum(0)
        plane = plane.reshape(nh, nl, rows, part).transpose(1, 0, 2, 3)
        plane = jnp.broadcast_to(plane[None], (nh,) + plane.shape).reshape(nz, nh * rows, part)
        piece = exchange(plane, ("h", "l")).sum(0).reshape(nh, 2, own, part)
        squares = lax.all_gather((piece * piece).sum((0, 2)), "c").sum(0)
        squares = squares.reshape(2, 2, part // 2).sum(1).reshape(1, part)
        piece = lax.dynamic_index_in_dim(piece, at_h, 0, keepdims=False)
        packed = jnp.concatenate([piece.reshape(rows, part), squares], 0).reshape(1, -1)
        packed = to_all(packed, ("x", "y", "l"), nx * ny * nl)
        grad_ms = packed[:, 0, rows * part :].reshape(-1, 2, part // 2).sum((0, 2)) / (rows_all * width)
        packed = packed.reshape(nx, ny * nl, -1)
        own_grads = lax.dynamic_index_in_dim(packed, at_yl, 1, keepdims=False)[:, : rows * part]
        own_grads = own_grads.reshape(nx, 2, own, part).transpose(2, 1, 0, 3).reshape(own, 2, width)
        ratio = jnp.sqrt(weight_ms) / jnp.sqrt(grad_ms + 1e-06)
        own_weights = own_weights.reshape(own, nx, 2, part).transpose(0, 2, 1, 3).reshape(own, 2, width)
        return own_weights - 0.5 * ratio[None, :, None] * own_grads

    return body


def solution(mesh):
    nx, ny, nh, nl, nc = mesh.shape["dp"], 4, 4, 4, 2
    grid = Mesh(mesh.devices.reshape(nx, ny, nh, nl, nc), ("x", "y", "h", "l", "c"))
    tokens = P("x", ("y", "h", "l", "c"), None)
    return jax.shard_map(
        make_body(nx, ny, nh, nl, nc),
        mesh=grid,
        in_specs=(tokens, tokens, tokens, tokens, P()),
        out_specs=P(("y", "h", "l", "c"), None, None),
        check_vma=False,
    )
```

```python
import functools

import jax
import jax.numpy as jnp
from jax import lax
from jax.experimental import pallas as pl
from jax.experimental.pallas import tpu as pltpu
from jax.sharding import Mesh, PartitionSpec as P

HEAD = 128
SCALE = HEAD ** (-0.5)
LOG2E = 1.4426950408889634
NT = (((1,), (1,)), ((), ()))
NN = (((1,), (0,)), ((), ()))
F32 = jnp.float32


def grads_kernel(
    ny, nz, core_ref, first_ref, low_hbm, q_hbm, d_hbm, lse_hbm, dot_hbm,
    send_ref, own_ref, sq_ref, own_w_ref,
    low_ref, q_ref, d_ref, lse_ref, dot_ref, w_ref, low_sem, row_sem, q_sem, d_sem,
):
    core = core_ref[0]
    groups, _, cols = q_ref.shape
    heads = cols // HEAD
    prefix_copy = pltpu.make_async_copy(low_hbm, low_ref, low_sem)
    row_copies = [
        pltpu.make_async_copy(lse_hbm, lse_ref, row_sem.at[0]),
        pltpu.make_async_copy(dot_hbm, dot_ref, row_sem.at[1]),
    ]

    def copies(g):
        span = pl.ds(g * cols, cols)
        return [
            pltpu.make_async_copy(q_hbm.at[:, span], q_ref.at[g], q_sem.at[g]),
            pltpu.make_async_copy(d_hbm.at[:, span], d_ref.at[g], d_sem.at[g]),
        ]

    prefix_copy.start()
    for copy in copies(0) + row_copies:
        copy.start()
    prefix_copy.wait()
    w_ref[...] = low_ref[...].astype(F32)
    start = pl.multiple_of(first_ref[0] * 8, 8)
    own_w_ref[...] = w_ref[pl.ds(start, own_w_ref.shape[0]), :]

    def gather(g, kv):
        rows = []
        for half in (1 - core, core):
            for y in range(ny):
                for r in range(2):
                    first = y * nz * 32 + half * 16 + r * 8 + g * 2 + kv
                    rows.append(w_ref[pl.ds(first, nz, stride=32), :])
        return jnp.concatenate(rows, 0)

    def rows_of(ref, g):
        return jnp.concatenate([ref[g, :, h * HEAD : (h + 1) * HEAD] for h in range(heads)], 0)

    def line_of(ref, g):
        lines = ref[pl.ds(g * heads, heads), :]
        return jnp.concatenate([lines[h : h + 1, :] for h in range(heads)], 1)

    def group(g, keys, values, stable):
        scores = lax.dot_general(keys, rows_of(q_ref, g), NT, preferred_element_type=F32)
        dprobs = lax.dot_general(values, rows_of(d_ref, g), NT, preferred_element_type=F32)
        lse = line_of(lse_ref, g) * LOG2E
        top = lse
        if stable:
            top = jnp.maximum(jnp.max(scores, axis=0, keepdims=True) * (SCALE * LOG2E), lse)
        probs = jnp.exp2(scores * (SCALE * LOG2E) - top)
        total = jnp.sum(probs, axis=0, keepdims=True)
        probs = probs * (1.0 / (total + (jnp.exp2(lse - top) if stable else 1.0)))
        dscores = (probs * (dprobs - line_of(dot_ref, g))).astype(jnp.bfloat16)
        probs = probs.astype(jnp.bfloat16)
        grad_v = lax.dot_general(probs, rows_of(d_ref, g), NN, preferred_element_type=F32)
        grad_k = lax.dot_general(dscores, rows_of(q_ref, g), NN, preferred_element_type=F32) * SCALE
        at = 0
        for ref in (send_ref, own_ref):
            for y in range(ny):
                for r in range(2):
                    ref[g, y, pl.ds(r, nz, stride=4), :] = grad_k[at : at + nz]
                    ref[g, y, pl.ds(2 + r, nz, stride=4), :] = grad_v[at : at + nz]
                    at += nz
        return total

    sides = []
    for kv in range(2):
        sides.append([gather(g, kv) for g in range(groups)])
        sq_ref[kv] = sum((x * x).reshape(-1, 8, HEAD).sum(0) for x in sides[kv])
    for copy in row_copies:
        copy.wait()
    peak = None
    for g in range(groups):
        for copy in copies(g):
            copy.wait()
        if g + 1 < groups:
            for copy in copies(g + 1):
                copy.start()
        keys, values = (sides[kv][g].astype(jnp.bfloat16) for kv in range(2))
        total = group(g, keys, values, False)
        peak = total if peak is None else jnp.maximum(peak, total)

    @pl.when(jnp.max(peak) > 2.0**100)
    def _():
        def again(g, carry):
            group(g, gather(g, 0).astype(jnp.bfloat16), gather(g, 1).astype(jnp.bfloat16), True)
            return carry

        lax.fori_loop(0, groups, again, 0)


def local_grads(nx, ny, nz, own, core, first, weights, queries, grad_out, seq_lse, out_dot):
    tok, cols = queries.shape
    half = jax.ShapeDtypeStruct((nx, ny, nz * 4, HEAD), F32)
    vmem = pl.BlockSpec(memory_space=pltpu.VMEM)
    smem = pl.BlockSpec(memory_space=pltpu.SMEM)
    hbm = pl.BlockSpec(memory_space=pltpu.HBM)
    operands = [weights, queries, grad_out, seq_lse, out_dot]
    operands = [pltpu.with_memory_space_constraint(x, pltpu.HBM) for x in operands]
    return pl.pallas_call(
        functools.partial(grads_kernel, ny, nz),
        in_specs=[smem, smem] + [hbm] * 5,
        out_specs=[vmem] * 4,
        out_shape=[half, half, jax.ShapeDtypeStruct((2, 8, HEAD), F32), jax.ShapeDtypeStruct((own * 8, HEAD), F32)],
        scratch_shapes=[
            pltpu.VMEM(weights.shape, weights.dtype),
            pltpu.VMEM((nx, tok, cols // nx), queries.dtype),
            pltpu.VMEM((nx, tok, cols // nx), grad_out.dtype),
            pltpu.VMEM(seq_lse.shape, F32),
            pltpu.VMEM(out_dot.shape, F32),
            pltpu.VMEM(weights.shape, F32),
            pltpu.SemaphoreType.DMA,
            pltpu.SemaphoreType.DMA((2,)),
            pltpu.SemaphoreType.DMA((nx,)),
            pltpu.SemaphoreType.DMA((nx,)),
        ],
        compiler_params=pltpu.CompilerParams(vmem_limit_bytes=40 * 2**20),
        name="prefix_grads",
    )(core.reshape(1), first.reshape(1), *operands)


def make_body(nx, ny, nh, nl, nc):
    nz = nh * nl

    def exchange(block, axes):
        return lax.all_to_all(block, axes, 0, 0, tiled=True)

    def to_all(block, axes, count):
        return exchange(jnp.broadcast_to(block[None], (count,) + block.shape), axes)

    def body(queries, grad_out, seq_lse, out_dot, prefix):
        rows_all, width = prefix.shape[0], prefix.shape[2]
        own = rows_all // (ny * nz * nc)
        part = width // nx
        core = lax.axis_index("c")
        first = lax.axis_index(("y", "h", "l", "c")) * own
        weights = prefix.reshape(rows_all, 2, nx, part).transpose(0, 2, 1, 3).reshape(-1, part)
        send, mine, w_squares, own_weights = local_grads(
            nx, ny, nz, own, core, first, weights,
            queries[0], grad_out[0], seq_lse[0].T, out_dot[0].T,
        )
        half = mine + lax.ppermute(send, "c", [(i, (i + 1) % nc) for i in range(nc)])
        weight_ms = w_squares.sum((1, 2)) / (rows_all * width)
        at_h = lax.axis_index("h").astype(jnp.uint32)
        at_c = core.astype(jnp.uint32)
        half, weight_ms, own_weights, at_h, at_c = lax.optimization_barrier(
            (half, weight_ms, own_weights, at_h, at_c)
        )
        rows = 2 * own
        plane = exchange(half.reshape(nx * ny, nz * rows, part), ("x", "y")).sum(0)
        plane = plane.reshape(nh, nl, rows, part).transpose(1, 0, 2, 3)
        plane = jnp.broadcast_to(plane[None], (nh,) + plane.shape).reshape(nz, nh * rows, part)
        piece = exchange(plane, ("h", "l")).sum(0).reshape(nh, 2, own, part)
        squares = (piece * piece).sum((0, 2))
        piece = lax.dynamic_index_in_dim(piece, at_h, 0, keepdims=False).reshape(rows, part)
        packed = to_all(jnp.concatenate([piece, squares, squares], 0), ("x", "c"), nx * nc)
        squares = packed[:, rows : rows + 2].sum(0)
        packed = packed[:, :rows].reshape(nx, nc, 2, own, part)
        own_grads = lax.dynamic_index_in_dim(packed, at_c, 1, keepdims=False)
        own_grads = own_grads.transpose(2, 1, 0, 3).reshape(own, 2, width)
        own_grads, squares = lax.optimization_barrier((own_grads, squares))
        grad_ms = to_all(squares, ("y", "l"), ny * nl).sum((0, 2)) / (rows_all * width)
        ratio = jnp.sqrt(weight_ms) / jnp.sqrt(grad_ms + 1e-06)
        own_weights = own_weights.reshape(own, nx, 2, part).transpose(0, 2, 1, 3).reshape(own, 2, width)
        return own_weights - 0.5 * ratio[None, :, None] * own_grads

    return body


def solution(mesh):
    nx, ny, nh, nl, nc = mesh.shape["dp"], 4, 4, 4, 2
    grid = Mesh(mesh.devices.reshape(nx, ny, nh, nl, nc), ("x", "y", "h", "l", "c"))
    tokens = P("x", ("y", "h", "l", "c"), None)
    return jax.shard_map(
        make_body(nx, ny, nh, nl, nc),
        mesh=grid,
        in_specs=(tokens, tokens, tokens, tokens, P()),
        out_specs=P(("y", "h", "l", "c"), None, None),
        check_vma=False,
    )
```
